256 devices in a mesh: ctx: 32 (over z, x), tp: 8 (over y, core).
Axes of the slice: x: 4, y: 4, z: 8, core: 2. Of those that a mesh axis runs over, the one named last changes fastest.
Arguments:
- query_vectors: bfloat16 [32768, 2048], P('ctx', 'tp'), may hold values from -160 to 160
- key_vectors: bfloat16 [32768, 2048], P('ctx', 'tp'), may hold values from -4 to 4
- value_vectors: bfloat16 [32768, 2048], P('ctx', 'tp'), may hold values from -6 to 6
- selections: int32 [64, 8, 8], P(None, 'tp'), may hold values from 0 to 63, as said below
- out_weight: bfloat16 [2048, 4096], P('tp'), may hold values from -0.125 to 0.125
Outputs:
- mixed_out: bfloat16 [32768, 4096], P(('ctx', 'tp'))
The draws below stay inside these ranges and needn't reach their ends.
Inputs may be any that keep to these rules, and one draw needn't show every extreme that they name: `selections`: entries below their query block's own index are distinct; an entry not below it selects nothing. An index of ctx holds 2 consecutive blocks; for each head group, the key blocks selected by the query blocks of one index lie on distinct indices, all below that index, so at most one key block of any index is selected by them.
All inputs are finite; a program needn't handle non-finite values.
Results may differ from the reference program's by a relative error of at most 0.019.
Values may be sent and summed in bfloat16 or wider, within the bound.
No kernel may reach another device: no remote copies, remote signals or barrier semaphores. Data moves between devices by JAX's collectives and lax.ppermute only.
A program may use at most 128 MiB of HBM per device.

```python
import math
import jax
import jax.numpy as jnp
from jax import lax

D = 4096
HEADS = 16
HD = 128
BLK = 512
SEL = 8
GH = 2
TOK_DEV = 1024
TOKENS = 32768
N_TP = 8


def draw_query_vectors(key, part):
    key = jax.random.fold_in(key, 1)
    fresh_rows = jnp.clip(jax.random.normal(key, (TOKENS, HEADS * HD)), -4.0, 4.0)
    return fresh_rows.astype(jnp.bfloat16)


def draw_key_vectors(key, part):
    key = jax.random.fold_in(key, 2)
    fresh_rows = jnp.clip(jax.random.normal(key, (TOKENS, HEADS * HD)), -4.0, 4.0)
    return fresh_rows.astype(jnp.bfloat16)


def draw_selections(key, part):
    key = jax.random.fold_in(key, 3)
    local_count = TOK_DEV // BLK
    device_count = TOKENS // TOK_DEV
    groups = HEADS // GH
    priority = jax.random.randint(jax.random.fold_in(key, 1), (device_count, groups, device_count), 0, 4096)
    source_ids = jnp.arange(device_count, dtype=jnp.int32)
    owner_ids = jnp.arange(device_count, dtype=jnp.int32)
    scores = priority * device_count + source_ids[None, None, :]
    eligible = source_ids[None, None, :] < owner_ids[:, None, None]
    scores = jnp.where(eligible, scores, -1 - source_ids[None, None, :])
    ranked = jnp.argsort(-scores, axis=-1, stable=True).astype(jnp.int32)
    slot_ids = jnp.arange(local_count, dtype=jnp.int32)[:, None] * SEL + jnp.arange(SEL, dtype=jnp.int32)[None, :]
    slot_clip = jnp.minimum(slot_ids, device_count - 1)
    chosen_dev = ranked[:, :, slot_clip]
    inner_pick = jax.random.randint(jax.random.fold_in(key, 2), (device_count, groups, local_count, SEL), 0, local_count)
    usable = slot_ids[None, None] < owner_ids[:, None, None, None]
    own_block = owner_ids[:, None] * local_count + jnp.arange(local_count, dtype=jnp.int32)[None, :]
    picked = jnp.where(usable, chosen_dev * local_count + inner_pick, own_block[:, None, :, None])
    return jnp.transpose(picked, (0, 2, 1, 3)).reshape(device_count * local_count, groups, SEL).astype(jnp.int32)


def shard_levels(stream_key, shape, pieces, least, largest):
    loudness = 1.0
    for axis_at, shards_of in pieces:
        draws = jax.random.uniform(jax.random.fold_in(jax.random.fold_in(stream_key, 6), axis_at), (shards_of,), jnp.float32, least / len(pieces), largest / len(pieces))
        loudness = loudness * jnp.repeat(jnp.exp(draws), shape[axis_at] // shards_of).reshape((-1,) + (1,) * (len(shape) - 1 - axis_at))
    return loudness


def noise(rng, shape, width, most, split=(), kind=jnp.bfloat16):
    result = width * jax.random.normal(rng, shape, jnp.float32)
    if split:
        result = result * shard_levels(rng, shape, split, -0.22, 0.18)
    return jnp.clip(result, -most, most).astype(kind)


def setup_inputs(seed: int = 0) -> dict:
    streams_of = jax.random.split(jax.random.key(seed), 6)
    return {
        "query_vectors": draw_query_vectors(jax.random.fold_in(streams_of[5], 71), 0),
        "key_vectors": draw_key_vectors(jax.random.fold_in(streams_of[5], 71), 0),
        "value_vectors": noise(streams_of[2], (TOKENS, HEADS * HD), 1.0, 6.0, ((0, 32), (1, 8))),
        "selections": draw_selections(jax.random.fold_in(streams_of[5], 71), 0),
        "out_weight": noise(streams_of[4], (HEADS * HD, D), (HEADS * HD) ** -0.5, 0.125, ((0, 8),)),
    }


NEG_FILL = -1e+30

def block_terms(query_blk, key_blk, value_blk, visible):
    scaling = 1.0 / math.sqrt(query_blk.shape[-1])
    scores = jnp.einsum('qhd,khd->hqk', query_blk.astype(jnp.float32), key_blk.astype(jnp.float32)) * scaling
    scores = jnp.where(visible, scores, NEG_FILL)
    maxima = lax.optimization_barrier(jnp.max(scores, axis=-1))
    weights = jnp.where(visible, jnp.exp(scores - maxima[..., None]), 0.0)
    totals = lax.optimization_barrier(jnp.sum(weights, axis=-1))
    rounded = lax.optimization_barrier(weights.astype(jnp.bfloat16))
    summed = jnp.einsum('hqk,khd->qhd', rounded.astype(jnp.float32), value_blk.astype(jnp.float32))
    return (lax.optimization_barrier(summed.astype(jnp.bfloat16)), maxima, totals)

def reference(query_vectors, key_vectors, value_vectors, selections, out_weight):
    blocks = TOKENS // BLK
    groups = HEADS // GH
    query_sets = query_vectors.reshape(blocks, BLK, groups, GH, HD)
    key_sets = key_vectors.reshape(blocks, BLK, groups, GH, HD)
    value_sets = value_vectors.reshape(blocks, BLK, groups, GH, HD)
    causal = jnp.tril(jnp.ones((BLK, BLK), dtype=bool))[None]

    def per_block(block_index):

        def per_group(group_index):
            query_group = query_sets[block_index, :, group_index]
            own_terms = block_terms(query_group, key_sets[block_index, :, group_index], value_sets[block_index, :, group_index], causal)
            chosen_ids = selections[block_index, group_index]
            valid_pick = chosen_ids < block_index
            safe_pick = jnp.where(valid_pick, chosen_ids, 0).astype(jnp.int32)
            key_chosen = key_sets[safe_pick, :, group_index]
            value_chosen = value_sets[safe_pick, :, group_index]

            def chosen_one(key_one, value_one, flag_one):
                return block_terms(query_group, key_one, value_one, flag_one)
            chosen_terms = jax.vmap(chosen_one)(key_chosen, value_chosen, valid_pick)
            all_sums = jnp.concatenate([own_terms[0][None], chosen_terms[0]], 0)
            all_max = jnp.concatenate([own_terms[1][None], chosen_terms[1]], 0)
            all_totals = jnp.concatenate([own_terms[2][None], chosen_terms[2]], 0)
            best_max = lax.optimization_barrier(jnp.max(all_max, axis=0))
            factor = jnp.exp(all_max - best_max[None])
            denominator = lax.optimization_barrier(jnp.sum(factor * all_totals, axis=0))
            numerator = lax.optimization_barrier(jnp.sum(jnp.swapaxes(factor, 1, 2)[..., None] * all_sums.astype(jnp.float32), axis=0))
            return (numerator / jnp.swapaxes(denominator, 0, 1)[..., None]).astype(jnp.bfloat16)
        grouped = lax.map(per_group, jnp.arange(groups, dtype=jnp.int32))
        return jnp.transpose(grouped, (1, 0, 2, 3)).reshape(BLK, HEADS * HD)
    attention = lax.map(per_block, jnp.arange(blocks, dtype=jnp.int32)).reshape(TOKENS, HEADS * HD)
    column_count = HEADS * HD // N_TP

    def add_term(part_index, running):
        first_column = part_index * column_count
        piece_cols = lax.dynamic_slice_in_dim(attention, first_column, column_count, 1)
        weight_rows = lax.dynamic_slice_in_dim(out_weight, first_column, column_count, 0)
        rounded = lax.optimization_barrier(jnp.dot(piece_cols, weight_rows, preferred_element_type=jnp.float32).astype(jnp.bfloat16))
        return running + rounded.astype(jnp.float32)
    term_sum = lax.fori_loop(0, N_TP, add_term, jnp.zeros((TOKENS, D), jnp.float32))
    return term_sum.astype(jnp.bfloat16)
```

```python
import functools
import math

import jax
import jax.numpy as jnp
from jax import lax
from jax.experimental import pallas as pl
from jax.experimental.pallas import tpu as pltpu
from jax.sharding import Mesh, PartitionSpec as P

HD = 128
BLK = 512
SEL = 8
GH = 2
NZ, NX, NY, NC = 8, 4, 4, 2
N_TP = NY * NC
LOCAL = 2
ROWS = LOCAL * BLK // N_TP
STAT = 16
MSG = GH * HD + STAT
D = 4096
NEG = -1e30
SCALE = math.log2(math.e) / math.sqrt(HD)
F32 = jnp.float32
BF16 = jnp.bfloat16


def dot(a, b, dims):
    return lax.dot_general(a, b, (dims, ((), ())), preferred_element_type=F32)


def attend_kernel(pos_ref, sel_ref, q_ref, k_ref, vt_ref, out_ref, acc, top, tot):
    my_z = pos_ref[0]
    my_x = pos_ref[1]

    def step(slot, query, diagonal):
        row0 = pl.multiple_of(slot * BLK, BLK)
        for head in range(GH):
            cols = pl.ds(head * HD, HD)
            scores = dot(k_ref[pl.ds(row0, BLK), cols], query[:, head * HD : (head + 1) * HD], ((1,), (1,)))
            scores = scores * SCALE
            if diagonal:
                key_at = lax.broadcasted_iota(jnp.int32, (BLK, BLK), 0)
                query_at = lax.broadcasted_iota(jnp.int32, (BLK, BLK), 1)
                scores = jnp.where(key_at <= query_at, scores, NEG)
            old = top[head]
            new = jnp.maximum(old, jnp.max(scores, axis=0, keepdims=True))
            fade = jnp.exp2(old - new)
            weights = jnp.exp2(scores - new)
            top[head] = new
            tot[head] = tot[head] * fade + jnp.sum(weights, axis=0, keepdims=True)
            z_at = slot // LOCAL
            vt = vt_ref[z_at, pl.ds(head * HD, HD), pl.ds(pl.multiple_of(slot % LOCAL * BLK, BLK), BLK)]
            acc[head] = acc[head] * fade + dot(vt, weights.astype(BF16), ((1,), (0,)))

    def query_block(index, carry):
        x_at = index // LOCAL
        half = index % LOCAL
        block = (my_z * NX + x_at) * LOCAL + half
        acc[...] = jnp.zeros_like(acc)
        top[...] = jnp.full_like(top, NEG)
        tot[...] = jnp.zeros_like(tot)
        query = q_ref[pl.ds(pl.multiple_of(index * BLK, BLK), BLK), :]

        @pl.when(x_at == my_x)
        def _():
            step(my_z * LOCAL + half, query, True)

        def pick(at, c):
            key = sel_ref[block * SEL + at]
            owner = key // LOCAL

            @pl.when((key < block) & (owner % NX == my_x))
            def _():
                step(owner // NX * LOCAL + key % LOCAL, query, False)

            return c

        lax.fori_loop(0, SEL, pick, 0)
        pieces = BLK // ROWS
        for head in range(GH):
            total = tot[head]
            some = total > 0.0
            safe = jnp.where(some, total, 1.0)
            mean = (acc[head] / safe).astype(BF16)
            log_total = jnp.where(some, top[head] + jnp.log2(safe), NEG)
            high = log_total.astype(BF16)
            rest = log_total - high.astype(F32)
            mid = rest.astype(BF16)
            low = (rest - mid.astype(F32)).astype(BF16)
            for piece in range(pieces):
                lanes = slice(piece * ROWS, (piece + 1) * ROWS)
                at = x_at * N_TP + half * pieces + piece
                out_ref[at, pl.ds(head * HD, HD), :] = mean[:, lanes]
                stats = jnp.concatenate(
                    [
                        jnp.broadcast_to(part[:, lanes].astype(F32), (8, ROWS))
                        for part in (high, mid, low)
                    ],
                    axis=0,
                )
                row = lax.broadcasted_iota(jnp.int32, (8, ROWS), 0)
                packed = jnp.where(row == 0, stats[0:8], jnp.where(row == 1, stats[8:16], stats[16:24]))
                if head == 0:
                    firsts = [packed] if piece == 0 else firsts + [packed]
                else:
                    both = jnp.concatenate([firsts[piece], packed], axis=0).astype(BF16)
                    out_ref[at, pl.ds(GH * HD, STAT), :] = both
        return carry

    lax.fori_loop(0, NX * LOCAL, query_block, 0)


def attend(pos, sel, query, key, value_t):
    vmem = pl.BlockSpec(memory_space=pltpu.VMEM)
    smem = pl.BlockSpec(memory_space=pltpu.SMEM)
    return pl.pallas_call(
        attend_kernel,
        out_shape=jax.ShapeDtypeStruct((NX * N_TP, MSG, ROWS), BF16),
        in_specs=[smem, smem, vmem, vmem, vmem],
        out_specs=vmem,
        scratch_shapes=[
            pltpu.VMEM((GH, HD, BLK), F32),
            pltpu.VMEM((GH, 1, BLK), F32),
            pltpu.VMEM((GH, 1, BLK), F32),
        ],
        compiler_params=pltpu.CompilerParams(vmem_limit_bytes=48 * 2**20),
        name="attend",
    )(pos, sel, query, key, value_t)


COLS = 512


def project_kernel(parts_ref, weight_ref, out_ref, held):
    @pl.when(pl.program_id(0) == 0)
    def _():
        for group in range(N_TP):
            for head in range(GH):
                logs = []
                for source in range(NX):
                    stats = parts_ref[source * N_TP + group, pl.ds(GH * HD, STAT), :].astype(F32)
                    own = stats[head * 8 : head * 8 + 8]
                    logs.append(own[0:1] + own[1:2] + own[2:3])
                best = functools.reduce(jnp.maximum, logs)
                shares = [jnp.exp2(one - best) for one in logs]
                inverse = 1.0 / functools.reduce(jnp.add, shares)
                total = jnp.zeros((HD, ROWS), F32)
                for source in range(NX):
                    part = parts_ref[source * N_TP + group, pl.ds(head * HD, HD), :]
                    total = total + part.astype(F32) * shares[source]
                held[:, pl.ds((group * GH + head) * HD, HD)] = (total * inverse).T.astype(BF16)

    out_ref[...] = dot(held[...], weight_ref[...], ((1,), (0,))).astype(BF16)


def project(parts, weight):
    depth = weight.shape[0]
    return pl.pallas_call(
        project_kernel,
        out_shape=jax.ShapeDtypeStruct((ROWS, D), BF16),
        grid=(D // COLS,),
        in_specs=[
            pl.BlockSpec(parts.shape, lambda n: (0, 0, 0)),
            pl.BlockSpec((depth, COLS), lambda n: (0, n)),
        ],
        out_specs=pl.BlockSpec((ROWS, COLS), lambda n: (0, n)),
        scratch_shapes=[pltpu.VMEM((ROWS, depth), BF16)],
        compiler_params=pltpu.CompilerParams(vmem_limit_bytes=32 * 2**20),
        name="project",
    )(parts, weight)


def local(query, key, value, selections, out_weight):
    pos = jnp.stack([lax.axis_index("z"), lax.axis_index("x")]).astype(jnp.int32)
    keys = lax.all_gather(key, "z", tiled=True)
    values_t = lax.all_gather(value.T, "z")
    queries = lax.all_gather(query, "x", tiled=True)
    weight = lax.all_gather(out_weight, ("y", "c"), tiled=True)
    parts = attend(pos, selections.reshape(-1), queries, keys, values_t)
    parts = lax.all_to_all(parts, ("x", "y", "c"), split_axis=0, concat_axis=0, tiled=True)
    return project(parts, weight)


def solution(mesh):
    grid = Mesh(mesh.devices.reshape(NZ, NX, NY, NC), ("z", "x", "y", "c"))
    tokens = P(("z", "x"), ("y", "c"))
    in_specs = (tokens, tokens, tokens, P(None, ("y", "c"), None), P(("y", "c"), None))
    out_specs = P(("z", "x", "y", "c"), None)
    return jax.shard_map(local, mesh=grid, in_specs=in_specs, out_specs=out_specs, check_vma=False)
```

```python
import functools
import math

import jax
import jax.numpy as jnp
from jax import lax
from jax.experimental import pallas as pl
from jax.experimental.pallas import tpu as pltpu
from jax.sharding import Mesh, PartitionSpec as P

HD = 128
BLK = 512
SEL = 8
GH = 2
NZ, NX, NY, NC = 8, 4, 4, 2
N_TP = NY * NC
LOCAL = 2
TOK = LOCAL * BLK
ROWS = TOK // N_TP
STAT = 16
MSG = HD + STAT
D = 4096
NEG = -1e30
SCALE = math.log2(math.e) / math.sqrt(HD)
F32 = jnp.float32
BF16 = jnp.bfloat16

UP = (0, 1, 0, 1, 0, 1, 0, 3, 2, 3, 2, 3, 2, 3)
DOWN = (1, 0, 1, 0, 1, 0, 1, 2, 3, 2, 3, 2, 3, 2)


def dot(a, b, dims):
    return lax.dot_general(a, b, (dims, ((), ())), preferred_element_type=F32)


def split_kernel(k_ref, v_ref, *outs):
    for head in range(GH):
        cols = pl.ds(head * HD, HD)
        outs[2 * head][...] = k_ref[:, cols]
        outs[2 * head + 1][...] = v_ref[:, cols].T


def split_heads(key, value):
    vmem = pl.BlockSpec(memory_space=pltpu.VMEM)
    shapes = [jax.ShapeDtypeStruct((TOK, HD), BF16), jax.ShapeDtypeStruct((HD, TOK), BF16)] * GH
    return pl.pallas_call(
        split_kernel,
        out_shape=shapes,
        in_specs=[vmem, vmem],
        out_specs=[vmem] * len(shapes),
        name="split_heads",
    )(key, value)


def attend_kernel(head, planes, offsets_k, offsets_v, pos_ref, sel_ref, *refs):
    count_q = len(planes)
    queries, refs = refs[:count_q], refs[count_q:]
    keys, refs = refs[:NZ], refs[NZ:]
    values, refs = refs[:NZ], refs[NZ:]
    out_ref, q_buf, k_buf, v_buf, stage, acc, top, tot, listed, sems, out_sems = refs[-11:]
    my_z = pos_ref[0]
    my_x = pos_ref[1]
    copies = []
    for at, ref in enumerate(queries):
        copies.append(pltpu.make_async_copy(ref.at[:, pl.ds(head * HD, HD)], q_buf.at[at], sems.at[at]))
    for at, (off, ref) in enumerate(zip(offsets_k, keys)):
        slot = lax.rem(my_z + NZ - off, NZ)
        copies.append(pltpu.make_async_copy(ref, k_buf.at[slot], sems.at[count_q + at]))
    for at, (off, ref) in enumerate(zip(offsets_v, values)):
        slot = lax.rem(my_z + NZ - off, NZ)
        copies.append(pltpu.make_async_copy(ref, v_buf.at[slot], sems.at[count_q + NZ + at]))
    for copy in copies:
        copy.start()
    for copy in copies:
        copy.wait()

    def step(slots, query, diagonal):
        places = [(slot // LOCAL, pl.multiple_of(slot % LOCAL * BLK, BLK)) for slot in slots]
        scores = [dot(k_buf[z_at, pl.ds(first, BLK), :], query, ((1,), (1,))) for z_at, first in places]
        if diagonal:
            key_at = lax.broadcasted_iota(jnp.int32, (BLK, BLK), 0)
            query_at = lax.broadcasted_iota(jnp.int32, (BLK, BLK), 1)
            scores[0] = jnp.where(key_at <= query_at, scores[0], NEG)
        old = top[...]
        new = functools.reduce(jnp.maximum, [old] + [jnp.max(one, axis=0, keepdims=True) for one in scores])
        fade = jnp.exp2((old - new) * SCALE)
        top[...] = new
        both = None
        for one, (z_at, first) in zip(scores, places):
            weights = jnp.exp2((one - new) * SCALE).astype(BF16)
            value = jnp.concatenate([v_buf[z_at, :, pl.ds(first, BLK)], jnp.ones((16, BLK), BF16)], axis=0)
            more = dot(value, weights, ((1,), (0,)))
            both = more if both is None else both + more
        tot[...] = tot[...] * fade + both[HD : HD + 1]
        acc[...] = acc[...] * fade + both[:HD]

    def query_block(index, carry):
        plane = index // LOCAL
        half = index % LOCAL
        x_at = lax.rem(my_x + NX - planes[0] - plane, NX)
        block = (my_z * NX + x_at) * LOCAL + half
        acc[...] = jnp.zeros_like(acc)
        top[...] = jnp.full_like(top, NEG)
        tot[...] = jnp.zeros_like(tot)
        query = q_buf[plane, pl.ds(pl.multiple_of(half * BLK, BLK), BLK), :]

        def gather(at, count):
            key = sel_ref[block * SEL + at]
            owner = key // LOCAL
            found = (key < block) & (owner % NX == my_x)
            listed[count] = owner // NX * LOCAL + key % LOCAL
            return count + found.astype(jnp.int32)

        count = lax.fori_loop(0, SEL, gather, 0)

        @pl.when(x_at == my_x)
        def _():
            step([my_z * LOCAL + half], query, True)

        def pairs(at, c):
            step([listed[2 * at], listed[2 * at + 1]], query, False)
            return c

        lax.fori_loop(0, count // 2, pairs, 0)

        @pl.when(count % 2 == 1)
        def _():
            step([listed[count - 1]], query, False)

        pieces = BLK // ROWS
        total = tot[...]
        some = total > 0.0
        safe = jnp.where(some, total, 1.0)
        mean = (acc[...] / safe).astype(BF16)
        log_total = jnp.where(some, top[...] * SCALE + jnp.log2(safe), NEG)
        high = log_total.astype(BF16).astype(F32)
        rest = log_total - high
        mid = rest.astype(BF16).astype(F32)
        low = rest - mid
        row = lax.broadcasted_iota(jnp.int32, (STAT, BLK), 0)
        wide = (STAT, BLK)
        packed = jnp.where(
            row == 0,
            jnp.broadcast_to(high, wide),
            jnp.where(row == 1, jnp.broadcast_to(mid, wide), jnp.broadcast_to(low, wide)),
        ).astype(BF16)
        for piece in range(pieces):
            lanes = slice(piece * ROWS, (piece + 1) * ROWS)
            at = index * pieces + piece
            stage[at, pl.ds(0, HD), :] = mean[:, lanes]
            stage[at, pl.ds(HD, STAT), :] = packed[:, lanes]
        return carry

    lax.fori_loop(0, count_q * LOCAL, query_block, 0)
    copies = []
    for plane, off in enumerate(planes):
        to = out_ref.at[pl.ds(lax.rem(my_x + NX - off, NX) * N_TP, N_TP)]
        copies.append(pltpu.make_async_copy(stage.at[pl.ds(plane * N_TP, N_TP)], to, out_sems.at[plane]))
    for copy in copies:
        copy.start()
    for copy in copies:
        copy.wait()


def attend(head, planes, pos, sel, queries, keys, values, parts=None):
    smem = pl.BlockSpec(memory_space=pltpu.SMEM)
    far = pl.BlockSpec(memory_space=pltpu.HBM)
    offsets_k, keys = zip(*keys)
    offsets_v, values = zip(*values)
    arrays = [queries[at] for at in planes] + [*keys, *values] + ([] if parts is None else [parts])
    arrays = [pltpu.with_memory_space_constraint(one, pltpu.HBM) for one in arrays]
    most = len(planes) * LOCAL * (SEL + 1) * BLK * BLK
    return pl.pallas_call(
        functools.partial(attend_kernel, head, planes, offsets_k, offsets_v),
        out_shape=jax.ShapeDtypeStruct((NX * N_TP, MSG, ROWS), BF16),
        in_specs=[smem, smem] + [far] * len(arrays),
        out_specs=far,
        scratch_shapes=[
            pltpu.VMEM((len(planes), TOK, HD), BF16),
            pltpu.VMEM((NZ, TOK, HD), BF16),
            pltpu.VMEM((NZ, HD, TOK), BF16),
            pltpu.VMEM((len(planes) * N_TP, MSG, ROWS), BF16),
            pltpu.VMEM((HD, BLK), F32),
            pltpu.VMEM((1, BLK), F32),
            pltpu.VMEM((1, BLK), F32),
            pltpu.SMEM((SEL + 1,), jnp.int32),
            pltpu.SemaphoreType.DMA((len(planes) + 2 * NZ,)),
            pltpu.SemaphoreType.DMA((len(planes),)),
        ],
        input_output_aliases={} if parts is None else {1 + len(arrays): 0},
        compiler_params=pltpu.CompilerParams(vmem_limit_bytes=16 * 2**20),
        name=f"attend{head}",
        cost_estimate=pl.CostEstimate(flops=4 * HD * most, transcendentals=most, bytes_accessed=12 * 2**20),
    )(pos, sel, *arrays)


COLS = 1024


def project_kernel(has_base, parts_ref, weight_ref, *refs):
    base_ref = refs[0] if has_base else None
    out_ref, held = refs[-2:]

    @pl.when(pl.program_id(0) == 0)
    def _():
        for group in range(N_TP):
            logs = []
            for source in range(NX):
                stats = parts_ref[source * N_TP + group, pl.ds(HD, STAT), :].astype(F32)
                logs.append(stats[0:1] + stats[1:2] + stats[2:3])
            best = functools.reduce(jnp.maximum, logs)
            shares = [jnp.exp2(one - best) for one in logs]
            inverse = 1.0 / functools.reduce(jnp.add, shares)
            total = jnp.zeros((HD, ROWS), F32)
            for source in range(NX):
                part = parts_ref[source * N_TP + group, pl.ds(0, HD), :]
                total = total + part.astype(F32) * shares[source]
            held[:, pl.ds(group * HD, HD)] = (total * inverse).T.astype(BF16)

    result = dot(held[...], weight_ref[...].reshape(N_TP * HD, COLS), ((1,), (0,)))
    if has_base:
        result = base_ref[...] + result
    out_ref[...] = result.astype(out_ref.dtype)


def project(head, parts, weight, base, dtype):
    depth = N_TP * HD
    piece = pl.BlockSpec((ROWS, COLS), lambda n: (0, n))
    return pl.pallas_call(
        functools.partial(project_kernel, base is not None),
        out_shape=jax.ShapeDtypeStruct((ROWS, D), dtype),
        grid=(D // COLS,),
        in_specs=[
            pl.BlockSpec(parts.shape, lambda n: (0, 0, 0)),
            pl.BlockSpec((N_TP, 1, HD, COLS), lambda n: (0, head, 0, n)),
        ]
        + ([piece] if base is not None else []),
        out_specs=piece,
        scratch_shapes=[pltpu.VMEM((ROWS, depth), BF16)],
        compiler_params=pltpu.CompilerParams(vmem_limit_bytes=16 * 2**20),
        cost_estimate=pl.CostEstimate(flops=2 * ROWS * depth * D, transcendentals=0, bytes_accessed=12 * 2**20),
        name=f"project{head}",
    )(parts, pltpu.with_memory_space_constraint(weight, pltpu.HBM), *([base] if base is not None else []))


def send(array, axis, count, by):
    return lax.ppermute(array, axis, [(at, (at + by) % count) for at in range(count)])


def local(query, key, value, selections, out_weight):
    pos = jnp.stack([lax.axis_index("z"), lax.axis_index("x")]).astype(jnp.int32)
    sel = selections.reshape(-1)
    queries = [query] + [send(query, "x", NX, by) for by in range(1, NX)]
    weight = lax.all_gather(out_weight.reshape(GH, HD, D), ("y", "c"))
    arrays = split_heads(key, value)
    found = [{0: array} for array in arrays]
    sent = {1: [], -1: []}
    base = None

    def travel(first, last, after=None):
        for turn in range(first, last):
            for sign, turns in ((1, UP), (-1, DOWN)):
                at = turns[turn]
                step = 1 + turns[:turn].count(at)
                source = found[at][sign * (step - 1)]
                if step == 1 and turn > 1:
                    source = lax.optimization_barrier((source, sent[sign][-2]))[0]
                if after is not None:
                    source = lax.optimization_barrier((source, after))[0]
                moved = send(source, "z", NZ, sign)
                found[at][sign * step] = moved
                sent[sign].append(moved)

    def head_parts(head, planes, after=None, parts=None):
        keys, values = (list(found[2 * head + at].items()) for at in range(2))
        if after is not None:
            held = ([array for _, array in keys], after)
            keys = list(zip([off for off, _ in keys], lax.optimization_barrier(held)[0]))
        return attend(head, planes, pos, sel, queries, keys, values, parts)

    def swap(parts):
        return lax.all_to_all(parts, ("x", "y", "c"), split_axis=0, concat_axis=0, tiled=True)

    def turn(at):
        return [sent[sign][at] for sign in (1, -1)]

    travel(0, 4)
    travel(4, 5, queries[1:])
    travel(5, 10)
    parts = head_parts(0, (0, 1), turn(7))
    travel(10, 11, parts)
    travel(11, 12)
    parts = head_parts(0, (2, 3), turn(9), parts)
    travel(12, 13, parts)
    travel(13, 14)
    parts = lax.optimization_barrier((parts, turn(11)))[0]
    base = project(0, swap(parts), weight, None, F32)
    return project(1, swap(head_parts(1, (0, 1, 2, 3))), weight, base, BF16)


def solution(mesh):
    grid = Mesh(mesh.devices.reshape(NZ, NX, NY, NC), ("z", "x", "y", "c"))
    tokens = P(("z", "x"), ("y", "c"))
    in_specs = (tokens, tokens, tokens, P(None, ("y", "c"), None), P(("y", "c"), None))
    out_specs = P(("z", "x", "y", "c"), None)
    return jax.shard_map(local, mesh=grid, in_specs=in_specs, out_specs=out_specs, check_vma=False)
```

```python
import functools
import math

import jax
import jax.numpy as jnp
from jax import lax
from jax.experimental import pallas as pl
from jax.experimental.pallas import tpu as pltpu
from jax.sharding import Mesh, PartitionSpec as P

HD = 128
BLK = 512
SEL = 8
GH = 2
NZ, NX, NY, NC = 8, 4, 4, 2
N_TP = NY * NC
LOCAL = 2
TOK = LOCAL * BLK
ROWS = TOK // N_TP
STAT = 16
MSG = HD + STAT
D = 4096
FAR = (3, 4, 5)
HELD = HD + 8
NEG = -1e30
SCALE = math.log2(math.e) / math.sqrt(HD)
F32 = jnp.float32
BF16 = jnp.bfloat16

UP = (0, 1, 0, 1, 0, 1, 0, 3, 2, 3, 2, 3, 2, 3)
DOWN = (1, 0, 1, 0, 1, 0, 1, 2, 3, 2, 3, 2, 3, 2)


def dot(a, b, dims):
    return lax.dot_general(a, b, (dims, ((), ())), preferred_element_type=F32)


def split_kernel(k_ref, v_ref, *outs):
    for head in range(GH):
        cols = pl.ds(head * HD, HD)
        outs[2 * head][...] = k_ref[:, cols]
        outs[2 * head + 1][...] = v_ref[:, cols].T


def split_heads(key, value):
    vmem = pl.BlockSpec(memory_space=pltpu.VMEM)
    shapes = [jax.ShapeDtypeStruct((TOK, HD), BF16), jax.ShapeDtypeStruct((HD, TOK), BF16)] * GH
    return pl.pallas_call(
        split_kernel,
        out_shape=shapes,
        in_specs=[vmem, vmem],
        out_specs=[vmem] * len(shapes),
        name="split_heads",
    )(key, value)


def attend_kernel(head, planes, which, offsets_k, offsets_v, pos_ref, sel_ref, *refs):
    count_q, count_k = len(planes), len(offsets_k)
    queries, refs = refs[:count_q], refs[count_q:]
    keys, refs = refs[:count_k], refs[count_k:]
    values, refs = refs[:count_k], refs[count_k:]
    states, refs = (refs[:count_q], refs[count_q:]) if which == "far" else (None, refs)
    outs, refs = refs[:count_q], refs[count_q:]
    q_buf, k_buf, v_buf, acc, top, tot, listed, sems = refs
    my_z = pos_ref[0]
    my_x = pos_ref[1]
    copies = []
    for at, ref in enumerate(queries):
        copies.append(pltpu.make_async_copy(ref.at[:, pl.ds(head * HD, HD)], q_buf.at[at], sems.at[at]))
    for at, (off, ref) in enumerate(zip(offsets_k, keys)):
        slot = lax.rem(my_z + NZ - off, NZ)
        copies.append(pltpu.make_async_copy(ref, k_buf.at[slot], sems.at[count_q + at]))
    for at, (off, ref) in enumerate(zip(offsets_v, values)):
        slot = lax.rem(my_z + NZ - off, NZ)
        copies.append(pltpu.make_async_copy(ref, v_buf.at[slot], sems.at[count_q + count_k + at]))
    for copy in copies:
        copy.start()
    for copy in copies:
        copy.wait()

    def step(slots, query, diagonal):
        places = [(slot // LOCAL, pl.multiple_of(slot % LOCAL * BLK, BLK)) for slot in slots]
        scores = [dot(k_buf[z_at, pl.ds(first, BLK), :], query, ((1,), (1,))) for z_at, first in places]
        if diagonal:
            key_at = lax.broadcasted_iota(jnp.int32, (BLK, BLK), 0)
            query_at = lax.broadcasted_iota(jnp.int32, (BLK, BLK), 1)
            scores[0] = jnp.where(key_at <= query_at, scores[0], NEG)
        old = top[...]
        new = functools.reduce(jnp.maximum, [old] + [jnp.max(one, axis=0, keepdims=True) for one in scores])
        fade = jnp.exp2((old - new) * SCALE)
        top[...] = new
        both = None
        for one, (z_at, first) in zip(scores, places):
            weights = jnp.exp2((one - new) * SCALE).astype(BF16)
            value = jnp.concatenate([v_buf[z_at, :, pl.ds(first, BLK)], jnp.ones((16, BLK), BF16)], axis=0)
            more = dot(value, weights, ((1,), (0,)))
            both = more if both is None else both + more
        tot[...] = tot[...] * fade + both[HD : HD + 1]
        acc[...] = acc[...] * fade + both[:HD]

    def query_block(plane, half, carry):
        x_at = lax.rem(my_x + NX - planes[plane], NX)
        block = (my_z * NX + x_at) * LOCAL + half
        if which != "far":
            acc[...] = jnp.zeros_like(acc)
            top[...] = jnp.full_like(top, NEG)
            tot[...] = jnp.zeros_like(tot)
        else:
            acc[...] = states[plane][half, pl.ds(0, HD), :]
            top[...] = states[plane][half, pl.ds(HD, 1), :]
            tot[...] = states[plane][half, pl.ds(HD + 1, 1), :]
        lanes = pl.ds(pl.multiple_of(half * BLK, BLK), BLK)
        query = q_buf[plane, lanes, :]

        count = 0
        for at in range(SEL):
            key = sel_ref[block * SEL + at]
            owner = key // LOCAL
            found = (key < block) & (owner % NX == my_x)
            rise = my_z - owner // NX
            if which == "near":
                found = found & ((rise < FAR[0]) | (rise > FAR[-1]))
            if which == "far":
                found = found & (rise >= FAR[0]) & (rise <= FAR[-1])
            listed[count] = owner // NX * LOCAL + key % LOCAL
            count = count + found.astype(jnp.int32)
        if which != "far" and planes[plane] == 0:
            step([my_z * LOCAL + half], query, True)

        def pairs(at, c):
            step([listed[2 * at], listed[2 * at + 1]], query, False)
            return c

        lax.fori_loop(0, count // 2, pairs, 0)

        @pl.when(count % 2 == 1)
        def _():
            step([listed[count - 1]], query, False)

        if which == "near":
            outs[plane][half, pl.ds(0, HD), :] = acc[...]
            outs[plane][half, pl.ds(HD, 1), :] = top[...]
            outs[plane][half, pl.ds(HD + 1, 1), :] = tot[...]
            return carry

        total = tot[...]
        some = total > 0.0
        safe = jnp.where(some, total, 1.0)
        log_total = jnp.where(some, top[...] * SCALE + jnp.log2(safe), NEG)
        high = log_total.astype(BF16).astype(F32)
        rest = log_total - high
        mid = rest.astype(BF16).astype(F32)
        low = rest - mid
        row = lax.broadcasted_iota(jnp.int32, (STAT, BLK), 0)
        wide = (STAT, BLK)
        packed = jnp.where(
            row == 0,
            jnp.broadcast_to(high, wide),
            jnp.where(row == 1, jnp.broadcast_to(mid, wide), jnp.broadcast_to(low, wide)),
        )
        outs[plane][pl.ds(0, HD), lanes] = (acc[...] * (1.0 / safe)).astype(BF16)
        outs[plane][pl.ds(HD, STAT), lanes] = packed.astype(BF16)
        return carry

    for plane in range(count_q):
        lax.fori_loop(0, LOCAL, functools.partial(query_block, plane), 0)


def attend(head, planes, which, pos, sel, queries, keys, values, states=()):
    if which != "all":
        keys, values = ([one for one in both if (one[0] % NZ in FAR) == (which == "far")] for both in (keys, values))
    smem = pl.BlockSpec(memory_space=pltpu.SMEM)
    vmem = pl.BlockSpec(memory_space=pltpu.VMEM)
    offsets_k, keys = zip(*keys)
    offsets_v, values = zip(*values)
    arrays = [queries[at] for at in planes] + [*keys, *values]
    place = pltpu.HBM if head == 0 else pltpu.VMEM
    arrays = [pltpu.with_memory_space_constraint(one, place) for one in arrays]
    shape = jax.ShapeDtypeStruct((MSG, TOK), BF16)
    if which == "near":
        shape = jax.ShapeDtypeStruct((LOCAL, HELD, BLK), F32)
    most = len(planes) * LOCAL * len(keys) * BLK * BLK
    return pl.pallas_call(
        functools.partial(attend_kernel, head, planes, which, offsets_k, offsets_v),
        out_shape=[shape] * len(planes),
        in_specs=[smem, smem] + [pl.BlockSpec(memory_space=place)] * len(arrays) + [vmem] * len(states),
        out_specs=[vmem] * len(planes),
        scratch_shapes=[
            pltpu.VMEM((len(planes), TOK, HD), BF16),
            pltpu.VMEM((NZ, TOK, HD), BF16),
            pltpu.VMEM((NZ, HD, TOK), BF16),
            pltpu.VMEM((HD, BLK), F32),
            pltpu.VMEM((1, BLK), F32),
            pltpu.VMEM((1, BLK), F32),
            pltpu.SMEM((SEL + 1,), jnp.int32),
            pltpu.SemaphoreType.DMA((len(arrays),)),
        ],
        compiler_params=pltpu.CompilerParams(vmem_limit_bytes=20 * 2**20),
        name=f"{which}{head}",
        cost_estimate=pl.CostEstimate(flops=4 * HD * most, transcendentals=most, bytes_accessed=8 * 2**20),
    )(pos, sel, *arrays, *states)


def merge_kernel(*refs):
    parts, out_ref = refs[:-1], refs[-1]
    for head in range(GH):
        own = parts[head * NX : (head + 1) * NX]
        logs = []
        for part in own:
            stats = part[pl.ds(HD, STAT), :].astype(F32)
            logs.append(stats[0:1] + stats[1:2] + stats[2:3])
        best = functools.reduce(jnp.maximum, logs)
        shares = [jnp.exp2(one - best) for one in logs]
        inverse = 1.0 / functools.reduce(jnp.add, shares)
        total = jnp.zeros((HD, TOK), F32)
        for part, share in zip(own, shares):
            total = total + part[pl.ds(0, HD), :].astype(F32) * share
        total = (total * inverse).T.astype(BF16)
        for piece in range(N_TP):
            out_ref[piece, head] = total[piece * ROWS : (piece + 1) * ROWS]


def merge(parts):
    vmem = pl.BlockSpec(memory_space=pltpu.VMEM)
    return pl.pallas_call(
        merge_kernel,
        out_shape=jax.ShapeDtypeStruct((N_TP, GH, ROWS, HD), BF16),
        in_specs=[vmem] * len(parts),
        out_specs=vmem,
        compiler_params=pltpu.CompilerParams(vmem_limit_bytes=16 * 2**20),
        name="merge",
    )(*parts)


STRIPES = 8
COLS = D // STRIPES


def project_kernel(parts_ref, weight_ref, out_ref, held, sems):
    def fetch(at):
        cols = pl.ds(at * COLS, COLS)
        return pltpu.make_async_copy(weight_ref.at[:, cols], held.at[:, cols], sems.at[at])

    for at in range(STRIPES):
        fetch(at).start()
    rows = jnp.concatenate([parts_ref[group, head] for group in range(N_TP) for head in range(GH)], axis=1)
    for at in range(STRIPES):
        fetch(at).wait()
        cols = pl.ds(at * COLS, COLS)
        out_ref[:, cols] = dot(rows, held[:, cols], ((1,), (0,))).astype(BF16)


def project(parts, weight):
    vmem = pl.BlockSpec(memory_space=pltpu.VMEM)
    return pl.pallas_call(
        project_kernel,
        out_shape=jax.ShapeDtypeStruct((ROWS, D), BF16),
        in_specs=[vmem, pl.BlockSpec(memory_space=pltpu.HBM)],
        out_specs=vmem,
        scratch_shapes=[pltpu.VMEM(weight.shape, BF16), pltpu.SemaphoreType.DMA((STRIPES,))],
        compiler_params=pltpu.CompilerParams(vmem_limit_bytes=30 * 2**20),
        cost_estimate=pl.CostEstimate(flops=2 * ROWS * weight.size, transcendentals=0, bytes_accessed=17 * 2**20),
        name="project",
    )(parts, pltpu.with_memory_space_constraint(weight, pltpu.HBM))


def send(array, axis, count, by):
    return lax.ppermute(array, axis, [(at, (at + by) % count) for at in range(count)])


def local(query, key, value, selections, out_weight):
    pos = jnp.stack([lax.axis_index("z"), lax.axis_index("x")]).astype(jnp.int32)
    sel = selections.reshape(-1)
    queries = [query] + [send(query, "x", NX, by) for by in range(1, NX)]
    weight = lax.all_gather(out_weight, ("y", "c"), tiled=True)
    arrays = split_heads(key, value)
    found = [{0: array} for array in arrays]
    sent = {1: [], -1: []}
    base = None

    def travel(first, last, after=None):
        for turn in range(first, last):
            for sign, turns in ((1, UP), (-1, DOWN)):
                at = turns[turn]
                step = 1 + turns[:turn].count(at)
                source = found[at][sign * (step - 1)]
                if step == 1 and turn > 1:
                    source = lax.optimization_barrier((source, sent[sign][-2]))[0]
                if after is not None:
                    source = lax.optimization_barrier((source, after))[0]
                moved = send(source, "z", NZ, sign)
                found[at][sign * step] = moved
                sent[sign].append(moved)

    def work(head, planes, which, after=None, states=None):
        keys, values = (list(found[2 * head + at].items()) for at in range(2))
        if after is not None:
            held = ([array for _, array in keys], after)
            keys = list(zip([off for off, _ in keys], lax.optimization_barrier(held)[0]))
        states = [] if states is None else [states[by] for by in planes]
        return dict(zip(planes, attend(head, planes, which, pos, sel, queries, keys, values, states)))

    def home(parts):
        return [send(one, "x", NX, -by) if by else one for by, one in parts.items()]

    def turn(at):
        return [sent[sign][at] for sign in (1, -1)]

    travel(0, 6)
    travel(6, 7, queries[1:])
    travel(7, 10)
    parts = work(0, (2, 1), "all", turn(7))
    merged = home(parts)
    travel(10, 11, list(parts.values()))
    travel(11, 12)
    parts = work(0, (3, 0), "all", turn(9))
    merged += home(parts)
    travel(12, 13, list(parts.values()))
    travel(13, 14)
    last = None
    for planes in ((2,), (1, 3), (0,)):
        parts = work(1, planes, "all", last)
        merged += home(parts)
        last = list(parts.values())
    attention = lax.all_to_all(merge(merged), ("y", "c"), split_axis=0, concat_axis=0, tiled=True)
    return project(attention, weight)


def solution(mesh):
    grid = Mesh(mesh.devices.reshape(NZ, NX, NY, NC), ("z", "x", "y", "c"))
    tokens = P(("z", "x"), ("y", "c"))
    in_specs = (tokens, tokens, tokens, P(None, ("y", "c"), None), P(("y", "c"), None))
    out_specs = P(("z", "x", "y", "c"), None)
    return jax.shard_map(local, mesh=grid, in_specs=in_specs, out_specs=out_specs, check_vma=False)
```
